1024 devices in a mesh: row: 32 (over z_lo, x, core), col: 32 (over y, z_hi).
Axes of the slice: x: 4, y: 8, z: 16 (z_hi: 4, z_lo: 4; z = z_hi * 4 + z_lo), core: 2. Of those that a mesh axis runs over, the one named last changes fastest.
Arguments:
- tiles: bfloat16 [32, 32, 16, 256, 256], P('row', 'col'), may hold values from -0.0625 to 0.0625
- tile_rows: int32 [32, 32, 16], P('row', 'col'), may hold values from 0 to 31
- tile_cols: int32 [32, 32, 16], P('row', 'col'), may hold values from 0 to 31
- counts: int32 [32, 32], P('row', 'col'), may hold values from 8 to 16, as said below
- vectors: bfloat16 [262144, 16], P(('row', 'col')), may hold values from -6 to 6
- basis: bfloat16 [262144, 128], P(('row', 'col'))
Outputs:
- residual_block: float32 [262144, 16], P(('row', 'col'))
- correlations: float32 [128, 16], replicated
The draws below stay inside these ranges and needn't reach their ends.
Inputs may be any that keep to these rules, and one draw needn't show every extreme that they name: `counts`: some device has exactly 16 live slots and some device exactly 8; tiles in dead slots are to be ignored.
All inputs are finite; a program needn't handle non-finite values.
Results may differ from the reference program's by a relative error of at most 0.0003.
Values may be sent and summed in bfloat16 or wider, within the bound.
No kernel may reach another device: no remote copies, remote signals or barrier semaphores. Data moves between devices by JAX's collectives and lax.ppermute only.
A program may use at most 32 MiB of HBM per device.

```python
import jax
import jax.numpy as jnp
from jax import lax

TILE = 256
B = 16
KMAX = 16
P_SIZE = 256
N = 262144
ROW_TILES = 32
COL_TILES = 32
BASIS = 128
N_ROW = 32
N_COL = 32


def draw_counts(key, part):
    key = jax.random.fold_in(key, 11)
    key_a, key_b = jax.random.split(key)
    values = jax.random.randint(key_a, (N_ROW * N_COL,), KMAX // 2, KMAX + 1)
    order = jax.random.permutation(key_b, N_ROW * N_COL)
    values = values.at[order[0]].set(KMAX)
    values = values.at[order[1]].set(KMAX // 2)
    return values.reshape(N_ROW, N_COL).astype(jnp.int32)


def draw_basis(key, part):
    key = jax.random.fold_in(key, 23)
    pieces = N_ROW * N_COL
    piece_index = (jnp.arange(N, dtype=jnp.int32) // P_SIZE).astype(jnp.float32)
    rising = 1.0 + 2.0 * piece_index / max(pieces - 1, 1)
    raw = jax.random.normal(key, (N, BASIS), jnp.float32)
    values = raw * rising[:, None] / jnp.sqrt(jnp.float32(N))
    return values.astype(jnp.bfloat16)


def with_ends(entries, own_key, smallest, largest):
    index_at = [jax.random.randint(jax.random.fold_in(own_key, axis), (), 0, length) for axis, length in enumerate(entries.shape)]
    widest = entries.shape.index(max(entries.shape))
    neighbour = index_at[:widest] + [(index_at[widest] + 1) % entries.shape[widest]] + index_at[widest + 1:]
    return entries.at[tuple(index_at)].set(smallest).at[tuple(neighbour)].set(largest)


def level_of(key, dims, cuts, smallest, top_value):
    level, own = 1.0, jax.random.fold_in(key, 6)
    for dim, parts in cuts:
        heights = jnp.exp(jax.random.uniform(jax.random.fold_in(own, dim), (parts,), jnp.float32, smallest / len(cuts), top_value / len(cuts)))
        level = level * jnp.repeat(heights, dims[dim] // parts).reshape([-1 if axis == dim else 1 for axis in range(len(dims))])
    return level


def noise(own_key, extent, scale, bound, cuts=(), held_as=jnp.bfloat16):
    array = scale * jax.random.normal(own_key, extent, jnp.float32)
    if cuts:
        array = array * level_of(own_key, extent, cuts, -0.22, 0.18)
    return jnp.clip(array, -bound, bound).astype(held_as)


def setup_inputs(seed: int = 0) -> dict:
    streams_of = jax.random.split(jax.random.key(seed), 7)
    return {
        "tiles": noise(streams_of[0], (N_ROW, N_COL, KMAX, TILE, TILE), (2 * KMAX * TILE * TILE // P_SIZE) ** -0.5, 0.0625, ((0, 32), (1, 32))),
        "tile_rows": with_ends(jax.random.randint(streams_of[1], (N_ROW, N_COL, KMAX), 0, ROW_TILES), jax.random.fold_in(streams_of[1], 1), 0, ROW_TILES - 1).astype(jnp.int32),
        "tile_cols": with_ends(jax.random.randint(streams_of[2], (N_ROW, N_COL, KMAX), 0, COL_TILES), jax.random.fold_in(streams_of[2], 1), 0, COL_TILES - 1).astype(jnp.int32),
        "counts": draw_counts(jax.random.fold_in(streams_of[6], 71), 0),
        "vectors": noise(streams_of[4], (N, B), 1.0, 6.0, ((0, 1024),)),
        "basis": draw_basis(jax.random.fold_in(streams_of[6], 71), 0),
    }


def reference(tiles, tile_rows, tile_cols, counts, vectors, basis):
    per_piece = P_SIZE // TILE
    grid_rows = jnp.arange(N_ROW, dtype=jnp.int32)[:, None, None]
    grid_cols = jnp.arange(N_COL, dtype=jnp.int32)[None, :, None]
    row_start = grid_rows * (N_COL * P_SIZE) + tile_rows * TILE
    col_start = ((tile_cols // per_piece) * N_COL + grid_cols) * P_SIZE + (tile_cols % per_piece) * TILE
    live = (jnp.arange(KMAX, dtype=jnp.int32)[None, None, :] < counts[:, :, None]).astype(jnp.float32)
    flat_tiles = tiles.reshape(N_ROW * N_COL, KMAX, TILE, TILE)
    flat_rows = row_start.reshape(N_ROW * N_COL, KMAX)
    flat_cols = col_start.reshape(N_ROW * N_COL, KMAX)
    flat_live = live.reshape(N_ROW * N_COL, KMAX)
    offsets = jnp.arange(TILE, dtype=jnp.int32)

    def one_cell(total, items):
        cell_tiles, starts_r, starts_c, alive = items
        index_r = starts_r[:, None] + offsets[None, :]
        index_c = starts_c[:, None] + offsets[None, :]
        right = vectors[index_c].astype(jnp.float32)
        left = vectors[index_r].astype(jnp.float32)
        cell32 = cell_tiles.astype(jnp.float32)
        forward = jnp.einsum("kij,kjb->kib", cell32, right) * alive[:, None, None]
        backward = jnp.einsum("kji,kjb->kib", cell32, left) * alive[:, None, None]
        total = total.at[index_r].add(forward)
        total = total.at[index_c].add(backward)
        return total, None

    start = jnp.zeros((N, B), jnp.float32)
    hx, unused = lax.scan(one_cell, start, (flat_tiles, flat_rows, flat_cols, flat_live))
    basis32 = basis.astype(jnp.float32)
    correlations = jnp.dot(basis32.T, hx, precision=lax.Precision.HIGHEST)
    residual_block = hx - jnp.dot(basis32, correlations, precision=lax.Precision.HIGHEST)
    return residual_block, correlations
```

```python
import jax
import jax.numpy as jnp
from jax import lax
from jax.experimental import pallas as pl
from jax.experimental.pallas import tpu as pltpu
from jax.sharding import Mesh, PartitionSpec as P

AXES = ("zl", "x", "c", "y", "zh")
SIZES = (4, 4, 2, 8, 4)
ROW = ("zl", "x", "c")
VMEM = pl.BlockSpec(memory_space=pltpu.VMEM)
SMEM = pl.BlockSpec(memory_space=pltpu.SMEM)


def exchange_zh(pieces):
    return [
        lax.ppermute(piece, "zh", [(i, i ^ d) for i in range(4)])
        for d, piece in zip((1, 2, 3), pieces)
    ]


def share(piece, axes, count):
    return lax.all_to_all(jnp.broadcast_to(piece[None], (count,) + piece.shape), axes, 0, 0)


def tile_kernel(row_ids, col_ids, count, zh, tiles, column_part, row_part, row_terms, col_terms):
    row_terms[...] = jnp.zeros_like(row_terms)
    col_terms[...] = jnp.zeros_like(col_terms)
    live = count[0]
    for k in range(tiles.shape[0]):
        r = row_ids[k] ^ zh[0]
        c = col_ids[k]
        tile = tiles[k]
        keep = (k < live).astype(jnp.float32)
        forward = lax.dot_general(
            column_part[c], tile, (((1,), (1,)), ((), ())), preferred_element_type=jnp.float32
        )
        backward = lax.dot_general(
            row_part[r], tile, (((1,), (0,)), ((), ())), preferred_element_type=jnp.float32
        )
        row_terms[r] = row_terms[r] + forward * keep
        col_terms[c] = col_terms[c] + backward * keep


def on_device(tiles, tile_rows, tile_cols, counts, vectors, basis):
    block = tiles[0, 0]
    size = block.shape[1]
    width = vectors.shape[1]
    zh = lax.axis_index("zh")
    own = vectors.T
    near = exchange_zh([own, own, own])
    column_part = share(own, ROW, 32)
    row_part = share(jnp.stack([own] + near), "y", 8).reshape(32, width, size)
    partial = jax.ShapeDtypeStruct((32, width, size), jnp.float32)
    row_terms, col_terms = pl.pallas_call(
        tile_kernel,
        out_shape=(partial, partial),
        in_specs=[SMEM] * 4 + [VMEM] * 3,
        out_specs=(VMEM, VMEM),
        compiler_params=pltpu.CompilerParams(vmem_limit_bytes=24 * 2**20),
    )(
        tile_rows.reshape(-1),
        tile_cols.reshape(-1),
        counts.reshape(-1),
        zh.reshape(1),
        block,
        column_part,
        row_part,
    )
    along_y = lax.all_to_all(row_terms.reshape(8, 4, width, size), "y", 0, 0).sum(0)
    far = exchange_zh([along_y[1], along_y[2], along_y[3]])
    col_share = lax.all_to_all(col_terms, ROW, 0, 0).sum(0)
    combined = col_share + (along_y[0] + far[0]) + (far[1] + far[2])
    basis32 = basis.astype(jnp.float32)
    corr = jnp.dot(combined, basis32, precision=lax.Precision.HIGHEST)
    corr = share(corr, ("zl", "x"), 16).sum(0)
    corr = lax.psum(corr, "c")
    corr = share(corr, "y", 8).sum(0)
    other = exchange_zh([corr, corr, corr])
    corr = (corr + other[0]) + (other[1] + other[2])
    removed = lax.dot_general(
        corr, basis32, (((1,), (1,)), ((), ())), precision=lax.Precision.HIGHEST
    )
    return ((combined - removed).T, corr.T)


def solution(mesh):
    fine = Mesh(mesh.devices.reshape(SIZES), AXES)
    col = ("y", "zh")
    placed = (
        P(ROW, col, None, None, None),
        P(ROW, col, None),
        P(ROW, col, None),
        P(ROW, col),
        P(AXES, None),
        P(AXES, None),
    )
    return jax.shard_map(
        on_device,
        mesh=fine,
        in_specs=placed,
        out_specs=(P(AXES, None), P()),
        check_vma=False,
    )
```

```python
import jax
import jax.numpy as jnp
from jax import lax
from jax.experimental import pallas as pl
from jax.experimental.pallas import tpu as pltpu
from jax.sharding import Mesh, PartitionSpec as P

AXES = ("zl", "x", "c", "y", "zh")
SIZES = (4, 4, 2, 8, 4)
ROW = ("zl", "x", "c")
VMEM = pl.BlockSpec(memory_space=pltpu.VMEM)
SMEM = pl.BlockSpec(memory_space=pltpu.SMEM)
LOW = 111
PARAMS = pltpu.CompilerParams(vmem_limit_bytes=24 * 2**20)


def encode(terms):
    rows = lax.broadcasted_iota(jnp.int32, terms.shape, 0)
    top = jnp.max(jnp.abs(terms), axis=0, keepdims=True)
    power = jnp.floor(jnp.log2(jnp.maximum(top, 2.0**-LOW))) + 1.0
    power = jnp.maximum(power, -float(LOW))
    q = jnp.round(terms * jnp.exp2(14.0 - power))
    q = jnp.clip(q, -16383.0, 16383.0).astype(jnp.int32)
    stored = jnp.broadcast_to(power.astype(jnp.int32) + LOW, terms.shape)
    return (2 * q + ((stored >> rows) & 1)).astype(jnp.int16)


def decode(codes):
    codes = codes.astype(jnp.int32)
    rows = lax.broadcasted_iota(jnp.int32, codes.shape, 0)
    place = jnp.where(rows < 7, 1 << jnp.minimum(rows, 7), 0).astype(jnp.float32)
    power = jnp.sum((codes & 1).astype(jnp.float32) * place, axis=0, keepdims=True) - float(LOW)
    return (codes >> 1).astype(jnp.float32) * jnp.exp2(power - 14.0)


def tile_kernel(forward, row_ids, col_ids, count, zh, tiles, part, codes, sums):
    sums[...] = jnp.zeros_like(sums)
    live = count[0]
    for k in range(tiles.shape[0]):
        r = row_ids[k] ^ zh[0]
        c = col_ids[k]
        source, target, contract = (c, r, 1) if forward else (r, c, 0)
        product = lax.dot_general(
            part[source],
            tiles[k],
            (((1,), (contract,)), ((), ())),
            preferred_element_type=jnp.float32,
        )
        sums[target] = sums[target] + product * (k < live).astype(jnp.float32)

    def code(i, carry):
        codes[i] = encode(sums[i])
        return carry

    lax.fori_loop(0, sums.shape[0], code, 0, unroll=4)


def tile_products(forward, scalars, tiles, part):
    flops = 2 * part.shape[1] * tiles.size
    return pl.pallas_call(
        lambda *refs: tile_kernel(forward, *refs),
        out_shape=jax.ShapeDtypeStruct(part.shape, jnp.int16),
        in_specs=[SMEM] * 4 + [VMEM] * 2,
        out_specs=VMEM,
        scratch_shapes=[pltpu.VMEM(part.shape, jnp.float32)],
        compiler_params=PARAMS,
        cost_estimate=pl.CostEstimate(
            flops=flops, bytes_accessed=4 * tiles.size, transcendentals=0
        ),
    )(*scalars, tiles, part)


def near_kernel(codes, kept, sent):
    for d, (ref, at) in enumerate(((kept, 0), (sent, 0), (sent, 1), (kept, 1))):
        total = decode(codes[0, d])
        for source in range(1, codes.shape[0]):
            total = total + decode(codes[source, d])
        ref[at] = total


def sum_along_y(codes):
    half = jax.ShapeDtypeStruct((2,) + codes.shape[2:], jnp.float32)
    return pl.pallas_call(
        near_kernel,
        out_shape=(half, half),
        in_specs=[VMEM],
        out_specs=(VMEM, VMEM),
        compiler_params=PARAMS,
    )(codes)


def row_kernel(codes, total):
    def add(i, value):
        return value + decode(codes[i])

    total[...] = lax.fori_loop(1, codes.shape[0], add, decode(codes[0]), unroll=4)


def sum_along_row(codes):
    return pl.pallas_call(
        row_kernel,
        out_shape=jax.ShapeDtypeStruct(codes.shape[1:], jnp.float32),
        in_specs=[VMEM],
        out_specs=VMEM,
        compiler_params=PARAMS,
    )(codes)


def across(value, d):
    return lax.ppermute(value, "zh", [(i, i ^ d) for i in range(4)])


def share(piece, axes, count):
    return lax.all_to_all(jnp.broadcast_to(piece[None], (count,) + piece.shape), axes, 0, 0)


def on_device(tiles, tile_rows, tile_cols, counts, vectors, basis):
    block = tiles[0, 0]
    size = block.shape[1]
    width = vectors.shape[1]
    scalars = (
        tile_rows.reshape(-1),
        tile_cols.reshape(-1),
        counts.reshape(-1),
        lax.axis_index("zh").reshape(1),
    )
    own = vectors.T
    column_part = share(own, ROW, 32)
    pair = jnp.stack([own, across(own, 3)])
    other = across(pair, 1)
    four = jnp.stack([pair[0], other[0], other[1], pair[1]])
    four, column_part = lax.optimization_barrier((four, column_part))
    row_part = share(four, "y", 8).reshape(32, width, size)
    row_codes = tile_products(True, scalars, block, column_part)
    row_codes, row_part = lax.optimization_barrier((row_codes, row_part))
    along_y = lax.all_to_all(row_codes.reshape(8, 4, width, size), "y", 0, 0)
    col_codes = tile_products(False, scalars, block, row_part)
    along_y, col_codes = lax.optimization_barrier((along_y, col_codes))
    along_row = lax.all_to_all(col_codes, ROW, 0, 0)
    kept, sent = sum_along_y(along_y)
    kept = kept + across(sent, 1)
    row_share = kept[0] + across(kept[1], 3)
    combined = row_share + sum_along_row(along_row)
    basis32 = basis.astype(jnp.float32)
    corr = jnp.dot(combined, basis32, precision=lax.Precision.HIGHEST)
    corr = share(corr, ("x", "c"), 8).sum(0)
    corr = share(corr, "y", 8).sum(0)
    corr = share(corr, ("zl", "zh"), 16).sum(0)
    removed = lax.dot_general(
        corr, basis32, (((1,), (1,)), ((), ())), precision=lax.Precision.HIGHEST
    )
    return ((combined - removed).T, corr.T)


def solution(mesh):
    fine = Mesh(mesh.devices.reshape(SIZES), AXES)
    col = ("y", "zh")
    placed = (
        P(ROW, col, None, None, None),
        P(ROW, col, None),
        P(ROW, col, None),
        P(ROW, col),
        P(AXES, None),
        P(AXES, None),
    )
    return jax.shard_map(
        on_device,
        mesh=fine,
        in_specs=placed,
        out_specs=(P(AXES, None), P()),
        check_vma=False,
    )
```

```python
import jax
import jax.numpy as jnp
from jax import lax
from jax.experimental import pallas as pl
from jax.experimental.pallas import tpu as pltpu
from jax.sharding import Mesh, PartitionSpec as P

AXES = ("zl", "x", "c", "y", "zh")
SIZES = (4, 4, 2, 8, 4)
ROW = ("zl", "x", "c")
VMEM = pl.BlockSpec(memory_space=pltpu.VMEM)
SMEM = pl.BlockSpec(memory_space=pltpu.SMEM)
LOW = 111
PARAMS = pltpu.CompilerParams(vmem_limit_bytes=24 * 2**20)


def encode(terms):
    rows = lax.broadcasted_iota(jnp.int32, terms.shape, 0)
    top = jnp.max(jnp.abs(terms), axis=0, keepdims=True)
    power = jnp.floor(jnp.log2(jnp.maximum(top, 2.0**-LOW))) + 1.0
    power = jnp.maximum(power, -float(LOW))
    q = jnp.round(terms * jnp.exp2(14.0 - power))
    q = jnp.clip(q, -16383.0, 16383.0).astype(jnp.int32)
    stored = jnp.broadcast_to(power.astype(jnp.int32) + LOW, terms.shape)
    return (2 * q + ((stored >> rows) & 1)).astype(jnp.int16)


def decode(codes):
    codes = codes.astype(jnp.int32)
    rows = lax.broadcasted_iota(jnp.int32, codes.shape, 0)
    place = jnp.where(rows < 7, 1 << jnp.minimum(rows, 7), 0).astype(jnp.float32)
    power = jnp.sum((codes & 1).astype(jnp.float32) * place, axis=0, keepdims=True) - float(LOW)
    return (codes >> 1).astype(jnp.float32) * jnp.exp2(power - 14.0)


def products(forward, row_ids, col_ids, count, place, tiles, part, sums):
    sums[...] = jnp.zeros_like(sums)
    live = count[0]
    for k in range(tiles.shape[0]):
        r = row_ids[k] ^ place[0]
        c = ((col_ids[k] & 1) ^ place[1]) * (sums.shape[0] // 2) + (col_ids[k] >> 1)
        source, target, contract = (c, r, 1) if forward else (r, c, 0)
        product = lax.dot_general(
            part[source],
            tiles[k],
            (((1,), (contract,)), ((), ())),
            preferred_element_type=jnp.float32,
        )
        sums[target] = sums[target] + product * (k < live).astype(jnp.float32)


def forward_kernel(row_ids, col_ids, count, place, tiles, near, far, codes, part, sums):
    half = near.shape[0]
    part[:half] = near[...]
    part[half:] = far[...]
    products(True, row_ids, col_ids, count, place, tiles, part, sums)

    def code(i, carry):
        codes[i] = encode(sums[i])
        return carry

    lax.fori_loop(0, sums.shape[0], code, 0, unroll=4)


def backward_kernel(row_ids, col_ids, count, place, tiles, part, kept, codes, sums):
    half = kept.shape[0]
    products(False, row_ids, col_ids, count, place, tiles, part, sums)

    def code(i, carry):
        codes[i] = encode(sums[half + i])
        return carry

    kept[...] = sums[:half]
    lax.fori_loop(0, half, code, 0, unroll=4)


def cost(tiles):
    return pl.CostEstimate(
        flops=32 * tiles.size, bytes_accessed=4 * tiles.size, transcendentals=0
    )


def forward_products(scalars, tiles, near, far):
    whole = (2 * near.shape[0],) + near.shape[1:]
    return pl.pallas_call(
        forward_kernel,
        out_shape=jax.ShapeDtypeStruct(whole, jnp.int16),
        in_specs=[SMEM] * 4 + [VMEM] * 3,
        out_specs=VMEM,
        scratch_shapes=[pltpu.VMEM(whole, near.dtype), pltpu.VMEM(whole, jnp.float32)],
        compiler_params=PARAMS,
        cost_estimate=cost(tiles),
    )(*scalars, tiles, near, far)


def backward_products(scalars, tiles, part):
    half = (part.shape[0] // 2,) + part.shape[1:]
    return pl.pallas_call(
        backward_kernel,
        out_shape=(
            jax.ShapeDtypeStruct(half, jnp.float32),
            jax.ShapeDtypeStruct(half, jnp.int16),
        ),
        in_specs=[SMEM] * 4 + [VMEM] * 2,
        out_specs=(VMEM, VMEM),
        scratch_shapes=[pltpu.VMEM(part.shape, jnp.float32)],
        compiler_params=PARAMS,
        cost_estimate=cost(tiles),
    )(*scalars, tiles, part)


def merge_kernel(kept, codes, merged):
    def code(i, carry):
        merged[i] = encode(kept[i] + decode(codes[i]))
        return carry

    lax.fori_loop(0, kept.shape[0], code, 0, unroll=4)


def merge(kept, codes):
    return pl.pallas_call(
        merge_kernel,
        out_shape=jax.ShapeDtypeStruct(codes.shape, jnp.int16),
        in_specs=[VMEM, VMEM],
        out_specs=VMEM,
        compiler_params=PARAMS,
    )(kept, codes)


def stack_kernel(copies, refs, out):
    at = 0
    for ref in refs:
        pieces = [ref[...]] if len(ref.shape) == 2 else [ref[i] for i in range(ref.shape[0])]
        for piece in pieces:
            for j in range(copies):
                out[j, at] = piece
            at += 1


def stack(copies, *pieces):
    count = sum(1 if piece.ndim == 2 else piece.shape[0] for piece in pieces)
    return pl.pallas_call(
        lambda *refs: stack_kernel(copies, refs[:-1], refs[-1]),
        out_shape=jax.ShapeDtypeStruct(
            (copies, count) + pieces[0].shape[-2:], pieces[0].dtype
        ),
        in_specs=[VMEM] * len(pieces),
        out_specs=VMEM,
        compiler_params=PARAMS,
    )(*pieces)


def near_kernel(codes, kept, sent):
    for d, (ref, at) in enumerate(((kept, 0), (sent, 0), (sent, 1), (kept, 1))):
        total = decode(codes[0, d])
        for source in range(1, codes.shape[0]):
            total = total + decode(codes[source, d])
        ref[at] = total


def sum_along_y(codes):
    half = jax.ShapeDtypeStruct((2,) + codes.shape[2:], jnp.float32)
    return pl.pallas_call(
        near_kernel,
        out_shape=(half, half),
        in_specs=[VMEM],
        out_specs=(VMEM, VMEM),
        compiler_params=PARAMS,
    )(codes)


def row_kernel(codes, total):
    def add(i, value):
        return value + decode(codes[i])

    total[...] = lax.fori_loop(1, codes.shape[0], add, decode(codes[0]), unroll=4)


def sum_along_row(codes):
    return pl.pallas_call(
        row_kernel,
        out_shape=jax.ShapeDtypeStruct(codes.shape[1:], jnp.float32),
        in_specs=[VMEM],
        out_specs=VMEM,
        compiler_params=PARAMS,
    )(codes)


def across(value, d):
    return lax.ppermute(value, "zh", [(i, i ^ d) for i in range(4)])


def swap_cores(value):
    return lax.ppermute(value, "c", [(0, 1), (1, 0)])


def share(piece, axes, count):
    return lax.all_to_all(jnp.broadcast_to(piece[None], (count,) + piece.shape), axes, 0, 0)


def on_device(tiles, tile_rows, tile_cols, counts, vectors, basis):
    block = tiles[0, 0]
    size = block.shape[1]
    width = vectors.shape[1]
    scalars = (
        tile_rows.reshape(-1),
        tile_cols.reshape(-1),
        counts.reshape(-1),
        jnp.stack([lax.axis_index("zh"), lax.axis_index("c")]),
    )
    own = vectors.T
    near = share(own, ("zl", "x"), 16)
    far = swap_cores(near)
    third = across(own, 3)
    middle = across(stack(1, own, third)[0], 1)
    four = stack(8, own, middle, third)
    four, near = lax.optimization_barrier((four, near))
    row_part = lax.all_to_all(four, "y", 0, 0).reshape(32, width, size)
    row_codes = forward_products(scalars, block, near, far)
    row_codes, row_part = lax.optimization_barrier((row_codes, row_part))
    along_y = lax.all_to_all(row_codes.reshape(8, 4, width, size), "y", 0, 0)
    col_kept, col_sent = backward_products(scalars, block, row_part)
    col_codes = merge(col_kept, swap_cores(col_sent))
    kept, sent = sum_along_y(along_y)
    sent, col_codes = lax.optimization_barrier((sent, col_codes))
    along_row = lax.all_to_all(col_codes, ("zl", "x"), 0, 0)
    kept = kept + across(sent, 1)
    row_share = kept[0] + across(kept[1], 3)
    combined = row_share + sum_along_row(along_row)
    basis32 = basis.astype(jnp.float32)
    corr = jnp.dot(combined, basis32, precision=lax.Precision.HIGHEST)
    corr = share(corr, ("x", "c"), 8).sum(0)
    corr = share(corr, "y", 8).sum(0)
    corr = share(corr, ("zl", "zh"), 16).sum(0)
    removed = lax.dot_general(
        corr, basis32, (((1,), (1,)), ((), ())), precision=lax.Precision.HIGHEST
    )
    return ((combined - removed).T, corr.T)


def solution(mesh):
    fine = Mesh(mesh.devices.reshape(SIZES), AXES)
    col = ("y", "zh")
    placed = (
        P(ROW, col, None, None, None),
        P(ROW, col, None),
        P(ROW, col, None),
        P(ROW, col),
        P(AXES, None),
        P(AXES, None),
    )
    return jax.shard_map(
        on_device,
        mesh=fine,
        in_specs=placed,
        out_specs=(P(AXES, None), P()),
        check_vma=False,
    )
```

```python
import jax
import jax.numpy as jnp
from jax import lax
from jax.experimental import pallas as pl
from jax.experimental.pallas import tpu as pltpu
from jax.sharding import Mesh, PartitionSpec as P

AXES = ("zl", "x", "c", "y", "zh")
SIZES = (4, 4, 2, 8, 4)
ROW = ("zl", "x", "c")
VMEM = pl.BlockSpec(memory_space=pltpu.VMEM)
SMEM = pl.BlockSpec(memory_space=pltpu.SMEM)
LOW = 111
PARAMS = pltpu.CompilerParams(vmem_limit_bytes=24 * 2**20)


def encode(terms):
    rows = lax.broadcasted_iota(jnp.int32, terms.shape, 0)
    top = jnp.max(jnp.abs(terms), axis=0, keepdims=True)
    power = jnp.floor(jnp.log2(jnp.maximum(top, 2.0**-LOW))) + 1.0
    power = jnp.maximum(power, -float(LOW))
    q = jnp.round(terms * jnp.exp2(14.0 - power))
    q = jnp.clip(q, -16383.0, 16383.0).astype(jnp.int32)
    stored = jnp.broadcast_to(power.astype(jnp.int32) + LOW, terms.shape)
    return (2 * q + ((stored >> rows) & 1)).astype(jnp.int16)


def decode(codes):
    codes = codes.astype(jnp.int32)
    rows = lax.broadcasted_iota(jnp.int32, codes.shape, 0)
    place = jnp.where(rows < 7, 1 << jnp.minimum(rows, 7), 0).astype(jnp.float32)
    power = jnp.sum((codes & 1).astype(jnp.float32) * place, axis=0, keepdims=True) - float(LOW)
    return (codes >> 1).astype(jnp.float32) * jnp.exp2(power - 14.0)


def products(forward, ids, tiles, part, sums, held, arrived):
    count = tiles.shape[0]
    copies = [
        pltpu.make_async_copy(tiles.at[k], held.at[k], arrived.at[k]) for k in range(count)
    ]
    for copy in copies:
        copy.start()
    sums[...] = jnp.zeros_like(sums)
    for k in range(count):
        r, c = ids[0, k], ids[1, k]
        source, target, contract = (c, r, 1) if forward else (r, c, 0)
        copies[k].wait()
        product = lax.dot_general(
            part[source],
            held[k],
            (((1,), (contract,)), ((), ())),
            preferred_element_type=jnp.float32,
        )
        sums[target] = sums[target] + product * (k < ids[2, k]).astype(jnp.float32)


def gather_parts(refs, part):
    at = 0
    for ref in refs:
        for block in [ref] if len(ref.shape) == 3 else [ref.at[0], ref.at[1]]:
            part[at : at + block.shape[0]] = block[...]
            at += block.shape[0]


def forward_kernel(ids, tiles, near, far, codes, part, sums, held, arrived):
    gather_parts((near, far), part)
    products(True, ids, tiles, part, sums, held, arrived)

    def code(y, carry):
        for d in range(codes.shape[1]):
            codes[y, d] = encode(sums[d * codes.shape[0] + y])
        return carry

    lax.fori_loop(0, codes.shape[0], code, 0)


def backward_kernel(ids, tiles, line, middle, third, kept, codes, part, sums, held, arrived):
    half = kept.shape[0]
    gather_parts((line, middle, third), part)
    products(False, ids, tiles, part, sums, held, arrived)

    def code(i, carry):
        codes[i] = encode(sums[half + i])
        return carry

    lax.fori_loop(0, half, code, 0, unroll=4)
    kept[...] = sums[:half]


def tile_products(kernel, outs, ids, tiles, *parts):
    whole = (32,) + parts[0].shape[1:]
    return pl.pallas_call(
        kernel,
        out_shape=[jax.ShapeDtypeStruct(dims + whole[1:], kind) for dims, kind in outs],
        in_specs=[SMEM, pl.BlockSpec(memory_space=pltpu.HBM)] + [VMEM] * len(parts),
        out_specs=[VMEM] * len(outs),
        scratch_shapes=[
            pltpu.VMEM(whole, parts[0].dtype),
            pltpu.VMEM(whole, jnp.float32),
            pltpu.VMEM(tiles.shape, tiles.dtype),
            pltpu.SemaphoreType.DMA((tiles.shape[0],)),
        ],
        compiler_params=PARAMS,
        cost_estimate=pl.CostEstimate(
            flops=32 * tiles.size, bytes_accessed=4 * tiles.size, transcendentals=0
        ),
    )(ids, tiles, *parts)


def merge_kernel(kept, codes, merged):
    def code(i, carry):
        merged[i] = encode(kept[i] + decode(codes[i]))
        return carry

    lax.fori_loop(0, kept.shape[0], code, 0, unroll=4)


def merge(kept, codes):
    return pl.pallas_call(
        merge_kernel,
        out_shape=jax.ShapeDtypeStruct(codes.shape, jnp.int16),
        in_specs=[VMEM, VMEM],
        out_specs=VMEM,
        compiler_params=PARAMS,
    )(kept, codes)


def near_kernel(codes, kept, sent):
    for d, (ref, at) in enumerate(((kept, 0), (sent, 0), (sent, 1), (kept, 1))):
        total = decode(codes[0, d])
        for source in range(1, codes.shape[0]):
            total = total + decode(codes[source, d])
        ref[at] = total


def sum_along_y(codes):
    half = jax.ShapeDtypeStruct((2,) + codes.shape[2:], jnp.float32)
    return pl.pallas_call(
        near_kernel,
        out_shape=(half, half),
        in_specs=[VMEM],
        out_specs=(VMEM, VMEM),
        compiler_params=PARAMS,
    )(codes)


def exact_dot(values, basis):
    total = None
    for step in range(3):
        head = values.astype(jnp.bfloat16)
        product = jnp.dot(head, basis, preferred_element_type=jnp.float32)
        total = product if total is None else total + product
        values = values - head.astype(jnp.float32)
    return total


def corr_kernel(codes, near, far, own_basis, far_basis, total, corr):
    def add(i, value):
        return value + decode(codes[i])

    total[...] = near[...] + lax.fori_loop(1, codes.shape[0], add, decode(codes[0]), unroll=5)
    value = exact_dot(total[...], own_basis[...]) + exact_dot(far[...], far_basis[...])
    for i in range(corr.shape[0]):
        corr[i] = value


def local_corr(copies, codes, near, far, own_basis, far_basis):
    return pl.pallas_call(
        corr_kernel,
        out_shape=(
            jax.ShapeDtypeStruct(near.shape, jnp.float32),
            jax.ShapeDtypeStruct((copies, near.shape[0], own_basis.shape[1]), jnp.float32),
        ),
        in_specs=[VMEM] * 5,
        out_specs=(VMEM, VMEM),
        compiler_params=PARAMS,
    )(codes, near, far, own_basis, far_basis)


def pair_kernel(first, second, out):
    out[0] = first[...]
    out[1] = second[...]


def pair(first, second):
    return pl.pallas_call(
        pair_kernel,
        out_shape=jax.ShapeDtypeStruct((2,) + first.shape, first.dtype),
        in_specs=[VMEM, VMEM],
        out_specs=VMEM,
        compiler_params=PARAMS,
    )(first, second)


def across(value, d):
    return lax.ppermute(value, "zh", [(i, i ^ d) for i in range(4)])


def swap_cores(value):
    return lax.ppermute(value, "c", [(0, 1), (1, 0)])


def share(piece, axes, count):
    return lax.all_to_all(jnp.broadcast_to(piece[None], (count,) + piece.shape), axes, 0, 0)


def on_device(tiles, tile_rows, tile_cols, counts, vectors, basis):
    block = tiles[0, 0]
    slots, size = block.shape[:2]
    width = vectors.shape[1]
    rows, cols = tile_rows.reshape(-1), tile_cols.reshape(-1)
    ids = jnp.stack(
        [
            ((rows & 3) ^ lax.axis_index("zh")) * 8 + (rows >> 2),
            ((cols & 1) ^ lax.axis_index("c")) * 16 + (cols >> 1),
            jnp.broadcast_to(counts.reshape(1), (slots,)),
        ]
    )
    own = vectors.T
    far_basis = across(basis, 3)
    line = share(own, "y", 8)
    line, own, far_basis = lax.optimization_barrier((line, own, far_basis))
    third = across(line, 3)
    near = share(own, ("zl", "x"), 16)
    near, third = lax.optimization_barrier((near, third))
    middle = across(pair(line, third), 1)
    far = swap_cores(near)
    (row_codes,) = tile_products(
        forward_kernel, [((8, 4), jnp.int16)], ids, block, near, far
    )
    row_codes, middle = lax.optimization_barrier((row_codes, middle))
    along_y = lax.all_to_all(row_codes, "y", 0, 0)
    col_kept, col_sent = tile_products(
        backward_kernel,
        [((16,), jnp.float32), ((16,), jnp.int16)],
        ids,
        block,
        line,
        middle,
        third,
    )
    col_codes = merge(col_kept, swap_cores(col_sent))
    along_y, col_codes = lax.optimization_barrier((along_y, col_codes))
    along_row = lax.all_to_all(col_codes, ("zl", "x"), 0, 0)
    kept, sent = sum_along_y(along_y)
    kept = kept + across(sent, 1)
    share_here, corr = local_corr(8, along_row, kept[0], kept[1], basis, far_basis)
    combined = share_here + across(kept[1], 3)
    corr = lax.all_to_all(corr, ("x", "c"), 0, 0).sum(0)
    corr = share(corr, "y", 8).sum(0)
    corr = share(corr, ("zl", "zh"), 16).sum(0)
    removed = lax.dot_general(
        corr,
        basis.astype(jnp.float32),
        (((1,), (1,)), ((), ())),
        precision=lax.Precision.HIGHEST,
    )
    return ((combined - removed).T, corr.T)


def solution(mesh):
    fine = Mesh(mesh.devices.reshape(SIZES), AXES)
    col = ("y", "zh")
    placed = (
        P(ROW, col, None, None, None),
        P(ROW, col, None),
        P(ROW, col, None),
        P(ROW, col),
        P(AXES, None),
        P(AXES, None),
    )
    return jax.shard_map(
        on_device,
        mesh=fine,
        in_specs=placed,
        out_specs=(P(AXES, None), P()),
        check_vma=False,
    )
```

```python
import jax
import jax.numpy as jnp
from jax import lax
from jax.experimental import pallas as pl
from jax.experimental.pallas import tpu as pltpu
from jax.sharding import Mesh, PartitionSpec as P

AXES = ("zl", "x", "c", "y", "zh")
SIZES = (4, 4, 2, 8, 4)
ROW = ("zl", "x", "c")
VMEM = pl.BlockSpec(memory_space=pltpu.VMEM)
SMEM = pl.BlockSpec(memory_space=pltpu.SMEM)
LOW = 111
PARAMS = pltpu.CompilerParams(vmem_limit_bytes=24 * 2**20)


def encode(terms):
    rows = lax.broadcasted_iota(jnp.int32, terms.shape, 0)
    top = jnp.max(jnp.abs(terms), axis=0, keepdims=True)
    power = jnp.floor(jnp.log2(jnp.maximum(top, 2.0**-LOW))) + 1.0
    power = jnp.maximum(power, -float(LOW))
    q = jnp.round(terms * jnp.exp2(14.0 - power))
    q = jnp.clip(q, -16383.0, 16383.0).astype(jnp.int32)
    stored = jnp.broadcast_to(power.astype(jnp.int32) + LOW, terms.shape)
    return (2 * q + ((stored >> rows) & 1)).astype(jnp.int16)


def decode(codes):
    codes = codes.astype(jnp.int32)
    rows = lax.broadcasted_iota(jnp.int32, codes.shape, 0)
    place = jnp.where(rows < 7, 1 << jnp.minimum(rows, 7), 0).astype(jnp.float32)
    power = jnp.sum((codes & 1).astype(jnp.float32) * place, axis=0, keepdims=True) - float(LOW)
    return (codes >> 1).astype(jnp.float32) * jnp.exp2(power - 14.0)


def products(forward, ids, tiles, part, sums):
    sums[...] = jnp.zeros_like(sums)
    for k in range(tiles.shape[0]):
        r, c = ids[0, k], ids[1, k]
        source, target, contract = (c, r, 1) if forward else (r, c, 0)
        product = lax.dot_general(
            part[source],
            tiles[k],
            (((1,), (contract,)), ((), ())),
            preferred_element_type=jnp.float32,
        )
        sums[target] = sums[target] + product * (k < ids[2, k]).astype(jnp.float32)


def forward_kernel(ids, tiles, near, far, codes, part, sums):
    half = near.shape[0]
    part[:half] = near[...]
    part[half:] = far[...]
    products(True, ids, tiles, part, sums)

    def code(y, carry):
        for d in range(codes.shape[1]):
            codes[y, d] = encode(sums[y * codes.shape[1] + d])
        return carry

    lax.fori_loop(0, codes.shape[0], code, 0)


def backward_kernel(ids, tiles, part, kept, codes, sums):
    half = kept.shape[0]
    products(False, ids, tiles, part, sums)

    def code(i, carry):
        codes[i] = encode(sums[half + i])
        return carry

    lax.fori_loop(0, half, code, 0, unroll=4)
    kept[...] = sums[:half]


def tile_products(kernel, outs, scratch, ids, tiles, *parts):
    piece = parts[0].shape[1:]
    return pl.pallas_call(
        kernel,
        out_shape=[jax.ShapeDtypeStruct(dims + piece, kind) for dims, kind in outs],
        in_specs=[SMEM] + [VMEM] * (1 + len(parts)),
        out_specs=[VMEM] * len(outs),
        scratch_shapes=[pltpu.VMEM((32,) + piece, kind) for kind in scratch],
        compiler_params=PARAMS,
        cost_estimate=pl.CostEstimate(
            flops=32 * tiles.size, bytes_accessed=4 * tiles.size, transcendentals=0
        ),
    )(ids, tiles, *parts)


def merge_kernel(kept, codes, merged):
    def code(i, carry):
        merged[i] = encode(kept[i] + decode(codes[i]))
        return carry

    lax.fori_loop(0, kept.shape[0], code, 0, unroll=4)


def merge(kept, codes):
    return pl.pallas_call(
        merge_kernel,
        out_shape=jax.ShapeDtypeStruct(codes.shape, jnp.int16),
        in_specs=[VMEM, VMEM],
        out_specs=VMEM,
        compiler_params=PARAMS,
    )(kept, codes)


def near_kernel(codes, kept, sent):
    for d, (ref, at) in enumerate(((kept, 0), (sent, 0), (sent, 1), (kept, 1))):
        total = decode(codes[0, d])
        for source in range(1, codes.shape[0]):
            total = total + decode(codes[source, d])
        ref[at] = total


def sum_along_y(codes):
    half = jax.ShapeDtypeStruct((2,) + codes.shape[2:], jnp.float32)
    return pl.pallas_call(
        near_kernel,
        out_shape=(half, half),
        in_specs=[VMEM],
        out_specs=(VMEM, VMEM),
        compiler_params=PARAMS,
    )(codes)


def exact_dot(values, basis):
    total = None
    for step in range(3):
        head = values.astype(jnp.bfloat16)
        product = jnp.dot(head, basis, preferred_element_type=jnp.float32)
        total = product if total is None else total + product
        values = values - head.astype(jnp.float32)
    return total


def corr_kernel(codes, near, far, own_basis, far_basis, total, corr):
    def add(i, value):
        return value + decode(codes[i])

    total[...] = near[...] + lax.fori_loop(1, codes.shape[0], add, decode(codes[0]), unroll=5)
    value = exact_dot(total[...], own_basis[...]) + exact_dot(far[...], far_basis[...])
    for i in range(corr.shape[0]):
        corr[i] = value


def local_corr(copies, codes, near, far, own_basis, far_basis):
    return pl.pallas_call(
        corr_kernel,
        out_shape=(
            jax.ShapeDtypeStruct(near.shape, jnp.float32),
            jax.ShapeDtypeStruct((copies, near.shape[0], own_basis.shape[1]), jnp.float32),
        ),
        in_specs=[VMEM] * 5,
        out_specs=(VMEM, VMEM),
        compiler_params=PARAMS,
    )(codes, near, far, own_basis, far_basis)


def stack_kernel(copies, refs, out):
    at = 0
    for ref in refs:
        pieces = [ref[...]] if len(ref.shape) == 2 else [ref[i] for i in range(ref.shape[0])]
        for piece in pieces:
            for j in range(copies):
                out[j, at] = piece
            at += 1


def stack(copies, *pieces):
    count = sum(1 if piece.ndim == 2 else piece.shape[0] for piece in pieces)
    return pl.pallas_call(
        lambda *refs: stack_kernel(copies, refs[:-1], refs[-1]),
        out_shape=jax.ShapeDtypeStruct(
            (copies, count) + pieces[0].shape[-2:], pieces[0].dtype
        ),
        in_specs=[VMEM] * len(pieces),
        out_specs=VMEM,
        compiler_params=PARAMS,
    )(*pieces)


def across(value, d):
    return lax.ppermute(value, "zh", [(i, i ^ d) for i in range(4)])


def swap_cores(value):
    return lax.ppermute(value, "c", [(0, 1), (1, 0)])


def share(piece, axes, count):
    return lax.all_to_all(jnp.broadcast_to(piece[None], (count,) + piece.shape), axes, 0, 0)


def on_device(tiles, tile_rows, tile_cols, counts, vectors, basis):
    block = tiles[0, 0]
    slots, size = block.shape[:2]
    width = vectors.shape[1]
    rows, cols = tile_rows.reshape(-1), tile_cols.reshape(-1)
    ids = jnp.stack(
        [
            rows ^ lax.axis_index("zh"),
            ((cols & 1) ^ lax.axis_index("c")) * 16 + (cols >> 1),
            jnp.broadcast_to(counts.reshape(1), (slots,)),
        ]
    )
    own = vectors.T
    near = share(own, ("zl", "x"), 16)
    third = across(own, 3)
    middle = across(stack(1, own, third)[0], 1)
    near, third = lax.optimization_barrier((near, third))
    far = swap_cores(near)
    four = stack(8, own, middle, third)
    four, far = lax.optimization_barrier((four, far))
    row_part = lax.all_to_all(four, "y", 0, 0).reshape(32, width, size)
    (row_codes,) = tile_products(
        forward_kernel,
        [((8, 4), jnp.int16)],
        [jnp.bfloat16, jnp.float32],
        ids,
        block,
        near,
        far,
    )
    row_codes, row_part = lax.optimization_barrier((row_codes, row_part))
    along_y = lax.all_to_all(row_codes, "y", 0, 0)
    col_kept, col_sent = tile_products(
        backward_kernel,
        [((16,), jnp.float32), ((16,), jnp.int16)],
        [jnp.float32],
        ids,
        block,
        row_part,
    )
    far_basis = across(basis, 3)
    col_codes = merge(col_kept, swap_cores(col_sent))
    along_y, col_codes, far_basis = lax.optimization_barrier((along_y, col_codes, far_basis))
    along_row = lax.all_to_all(col_codes, ("zl", "x"), 0, 0)
    kept, sent = sum_along_y(along_y)
    kept = kept + across(sent, 1)
    share_here, corr = local_corr(8, along_row, kept[0], kept[1], basis, far_basis)
    combined = share_here + across(kept[1], 3)
    corr = lax.all_to_all(corr, ("x", "c"), 0, 0).sum(0)
    corr = share(corr, "y", 8).sum(0)
    corr = share(corr, ("zl", "zh"), 16).sum(0)
    removed = lax.dot_general(
        corr,
        basis.astype(jnp.float32),
        (((1,), (1,)), ((), ())),
        precision=lax.Precision.HIGHEST,
    )
    return ((combined - removed).T, corr.T)


def solution(mesh):
    fine = Mesh(mesh.devices.reshape(SIZES), AXES)
    col = ("y", "zh")
    placed = (
        P(ROW, col, None, None, None),
        P(ROW, col, None),
        P(ROW, col, None),
        P(ROW, col),
        P(AXES, None),
        P(AXES, None),
    )
    return jax.shard_map(
        on_device,
        mesh=fine,
        in_specs=placed,
        out_specs=(P(AXES, None), P()),
        check_vma=False,
    )
```

```python
import jax
import jax.numpy as jnp
from jax import lax
from jax.experimental import pallas as pl
from jax.experimental.pallas import tpu as pltpu
from jax.sharding import Mesh, PartitionSpec as P

AXES = ("zl", "x", "c", "y", "zh")
SIZES = (4, 4, 2, 8, 4)
ROW = ("zl", "x", "c")
VMEM = pl.BlockSpec(memory_space=pltpu.VMEM)
SMEM = pl.BlockSpec(memory_space=pltpu.SMEM)
LOW = 111
PARAMS = pltpu.CompilerParams(vmem_limit_bytes=24 * 2**20)


def encode(terms):
    rows = lax.broadcasted_iota(jnp.int32, terms.shape, 0)
    top = jnp.max(jnp.abs(terms), axis=0, keepdims=True)
    power = jnp.floor(jnp.log2(jnp.maximum(top, 2.0**-LOW))) + 1.0
    power = jnp.maximum(power, -float(LOW))
    q = jnp.round(terms * jnp.exp2(14.0 - power))
    q = jnp.clip(q, -16383.0, 16383.0).astype(jnp.int32)
    stored = jnp.broadcast_to(power.astype(jnp.int32) + LOW, terms.shape)
    return (2 * q + ((stored >> rows) & 1)).astype(jnp.int16)


def decode(codes):
    codes = codes.astype(jnp.int32)
    rows = lax.broadcasted_iota(jnp.int32, codes.shape, 0)
    place = jnp.where(rows < 7, 1 << jnp.minimum(rows, 7), 0).astype(jnp.float32)
    power = jnp.sum((codes & 1).astype(jnp.float32) * place, axis=0, keepdims=True) - float(LOW)
    return (codes >> 1).astype(jnp.float32) * jnp.exp2(power - 14.0)


def products(forward, ids, tiles, part, sums):
    sums[...] = jnp.zeros_like(sums)
    for k in range(tiles.shape[0]):
        r, c = ids[0, k], ids[1, k]
        source, target, contract = (c, r, 1) if forward else (r, c, 0)
        product = lax.dot_general(
            part[source],
            tiles[k],
            (((1,), (contract,)), ((), ())),
            preferred_element_type=jnp.float32,
        )
        sums[target] = sums[target] + product * (k < ids[2, k]).astype(jnp.float32)


def forward_kernel(ids, tiles, part, codes, sums):
    products(True, ids, tiles, part, sums)

    def code(y, carry):
        for d in range(codes.shape[1]):
            codes[y, d] = encode(sums[y * codes.shape[1] + d])
        return carry

    lax.fori_loop(0, codes.shape[0], code, 0)


def backward_kernel(ids, tiles, part, codes, sums):
    products(False, ids, tiles, part, sums)

    def code(i, carry):
        codes[i] = encode(sums[i])
        return carry

    lax.fori_loop(0, sums.shape[0], code, 0, unroll=4)


def tile_products(kernel, lead, ids, tiles, part):
    return pl.pallas_call(
        kernel,
        out_shape=jax.ShapeDtypeStruct(lead + part.shape[1:], jnp.int16),
        in_specs=[SMEM, VMEM, VMEM],
        out_specs=VMEM,
        scratch_shapes=[pltpu.VMEM(part.shape, jnp.float32)],
        compiler_params=PARAMS,
        cost_estimate=pl.CostEstimate(
            flops=32 * tiles.size, bytes_accessed=4 * tiles.size, transcendentals=0
        ),
    )(ids, tiles, part)


def near_kernel(codes, kept, sent):
    for d, (ref, at) in enumerate(((kept, 0), (sent, 0), (sent, 1), (kept, 1))):
        total = decode(codes[0, d])
        for source in range(1, codes.shape[0]):
            total = total + decode(codes[source, d])
        ref[at] = total


def sum_along_y(codes):
    half = jax.ShapeDtypeStruct((2,) + codes.shape[2:], jnp.float32)
    return pl.pallas_call(
        near_kernel,
        out_shape=(half, half),
        in_specs=[VMEM],
        out_specs=(VMEM, VMEM),
        compiler_params=PARAMS,
    )(codes)


def exact_dot(values, basis):
    total = None
    for step in range(3):
        head = values.astype(jnp.bfloat16)
        product = jnp.dot(head, basis, preferred_element_type=jnp.float32)
        total = product if total is None else total + product
        values = values - head.astype(jnp.float32)
    return total


def corr_kernel(codes, kept, own_basis, third_basis, total, corr):
    def add(i, value):
        return value + decode(codes[i])

    total[...] = kept[0] + lax.fori_loop(1, codes.shape[0], add, decode(codes[0]), unroll=4)
    value = exact_dot(total[...], own_basis[...]) + exact_dot(kept[1], third_basis[...])
    for i in range(corr.shape[0]):
        corr[i] = value


def local_corr(copies, codes, kept, *blocks):
    return pl.pallas_call(
        corr_kernel,
        out_shape=(
            jax.ShapeDtypeStruct(kept.shape[1:], jnp.float32),
            jax.ShapeDtypeStruct((copies, kept.shape[1], blocks[0].shape[1]), jnp.float32),
        ),
        in_specs=[VMEM] * 4,
        out_specs=(VMEM, VMEM),
        compiler_params=PARAMS,
    )(codes, kept, *blocks)


def stack_kernel(copies, refs, out):
    at = 0
    for ref in refs:
        pieces = [ref[...]] if len(ref.shape) == 2 else [ref[i] for i in range(ref.shape[0])]
        for piece in pieces:
            for j in range(copies):
                out[j, at] = piece
            at += 1


def stack(copies, *pieces):
    count = sum(1 if piece.ndim == 2 else piece.shape[0] for piece in pieces)
    return pl.pallas_call(
        lambda *refs: stack_kernel(copies, refs[:-1], refs[-1]),
        out_shape=jax.ShapeDtypeStruct(
            (copies, count) + pieces[0].shape[-2:], pieces[0].dtype
        ),
        in_specs=[VMEM] * len(pieces),
        out_specs=VMEM,
        compiler_params=PARAMS,
    )(*pieces)


def across(value, d):
    return lax.ppermute(value, "zh", [(i, i ^ d) for i in range(4)])


def share(piece, axes, count):
    return lax.all_to_all(jnp.broadcast_to(piece[None], (count,) + piece.shape), axes, 0, 0)


def on_device(tiles, tile_rows, tile_cols, counts, vectors, basis):
    block = tiles[0, 0]
    slots, size = block.shape[:2]
    width = vectors.shape[1]
    rows, cols = tile_rows.reshape(-1), tile_cols.reshape(-1)
    ids = jnp.stack(
        [
            rows ^ lax.axis_index("zh"),
            cols,
            jnp.broadcast_to(counts.reshape(1), (slots,)),
        ]
    )
    own = vectors.T
    column_part = share(own, ROW, 32)
    third = across(own, 3)
    middle = across(stack(1, own, third)[0], 1)
    third_basis = across(basis, 3)
    four = stack(8, own, middle, third)
    four, column_part = lax.optimization_barrier((four, column_part))
    row_part = lax.all_to_all(four, "y", 0, 0).reshape(32, width, size)
    row_codes = tile_products(forward_kernel, (8, 4), ids, block, column_part)
    row_codes, row_part, third_basis = lax.optimization_barrier(
        (row_codes, row_part, third_basis)
    )
    along_y = lax.all_to_all(row_codes, "y", 0, 0)
    col_codes = tile_products(backward_kernel, (32,), ids, block, row_part)
    along_y, col_codes = lax.optimization_barrier((along_y, col_codes))
    along_row = lax.all_to_all(col_codes, ROW, 0, 0)
    kept, sent = sum_along_y(along_y)
    kept = kept + across(sent, 1)
    total, corr = local_corr(8, along_row, kept, basis, third_basis)
    combined = total + across(kept[1], 3)
    corr = lax.all_to_all(corr, ("x", "c"), 0, 0).sum(0)
    corr = share(corr, "y", 8).sum(0)
    corr = share(corr, ("zl", "zh"), 16).sum(0)
    removed = lax.dot_general(
        corr,
        basis.astype(jnp.float32),
        (((1,), (1,)), ((), ())),
        precision=lax.Precision.HIGHEST,
    )
    return ((combined - removed).T, corr.T)


def solution(mesh):
    fine = Mesh(mesh.devices.reshape(SIZES), AXES)
    col = ("y", "zh")
    placed = (
        P(ROW, col, None, None, None),
        P(ROW, col, None),
        P(ROW, col, None),
        P(ROW, col),
        P(AXES, None),
        P(AXES, None),
    )
    return jax.shard_map(
        on_device,
        mesh=fine,
        in_specs=placed,
        out_specs=(P(AXES, None), P()),
        check_vma=False,
    )
```

```python
import jax
import jax.numpy as jnp
from jax import lax
from jax.experimental import pallas as pl
from jax.experimental.pallas import tpu as pltpu
from jax.sharding import Mesh, PartitionSpec as P

AXES = ("zl", "x", "c", "y", "zh")
SIZES = (4, 4, 2, 8, 4)
ROW = ("zl", "x", "c")
VMEM = pl.BlockSpec(memory_space=pltpu.VMEM)
SMEM = pl.BlockSpec(memory_space=pltpu.SMEM)
LOW = 111
PARAMS = pltpu.CompilerParams(vmem_limit_bytes=24 * 2**20)


def encode(terms):
    rows = lax.broadcasted_iota(jnp.int32, terms.shape, 0)
    top = jnp.max(jnp.abs(terms), axis=0, keepdims=True)
    power = jnp.floor(jnp.log2(jnp.maximum(top, 2.0**-LOW))) + 1.0
    power = jnp.maximum(power, -float(LOW))
    q = jnp.round(terms * jnp.exp2(14.0 - power))
    q = jnp.clip(q, -16383.0, 16383.0).astype(jnp.int32)
    stored = jnp.broadcast_to(power.astype(jnp.int32) + LOW, terms.shape)
    return (2 * q + ((stored >> rows) & 1)).astype(jnp.int16)


def decode(codes):
    codes = codes.astype(jnp.int32)
    rows = lax.broadcasted_iota(jnp.int32, codes.shape, 0)
    place = jnp.where(rows < 7, 1 << jnp.minimum(rows, 7), 0).astype(jnp.float32)
    power = jnp.sum((codes & 1).astype(jnp.float32) * place, axis=0, keepdims=True) - float(LOW)
    return (codes >> 1).astype(jnp.float32) * jnp.exp2(power - 14.0)


def products(forward, ids, tiles, part, sums):
    sums[...] = jnp.zeros_like(sums)
    for k in range(tiles.shape[0]):
        r, c = ids[0, k], ids[1, k]
        source, target, contract = (c, r, 1) if forward else (r, c, 0)
        product = lax.dot_general(
            part[source],
            tiles[k],
            (((1,), (contract,)), ((), ())),
            preferred_element_type=jnp.float32,
        )
        sums[target] = sums[target] + product * (k < ids[2, k]).astype(jnp.float32)


def forward_kernel(ids, tiles, part, codes, sums):
    products(True, ids, tiles, part, sums)

    def code(y, carry):
        for d in range(codes.shape[1]):
            codes[y, d] = encode(sums[y * codes.shape[1] + d])
        return carry

    lax.fori_loop(0, codes.shape[0], code, 0)


def backward_kernel(ids, tiles, part, codes, sums):
    products(False, ids, tiles, part, sums)

    def code(i, carry):
        codes[i] = encode(sums[i])
        return carry

    lax.fori_loop(0, sums.shape[0], code, 0, unroll=4)


def tile_products(kernel, lead, ids, tiles, part):
    return pl.pallas_call(
        kernel,
        out_shape=jax.ShapeDtypeStruct(lead + part.shape[1:], jnp.int16),
        in_specs=[SMEM, VMEM, VMEM],
        out_specs=VMEM,
        scratch_shapes=[pltpu.VMEM(part.shape, jnp.float32)],
        compiler_params=PARAMS,
        cost_estimate=pl.CostEstimate(
            flops=32 * tiles.size, bytes_accessed=4 * tiles.size, transcendentals=0
        ),
    )(ids, tiles, part)


def near_kernel(codes, kept, sent):
    for d, (ref, at) in enumerate(((kept, 0), (sent, 0), (sent, 1), (kept, 1))):
        total = decode(codes[0, d])
        for source in range(1, codes.shape[0]):
            total = total + decode(codes[source, d])
        ref[at] = total


def sum_along_y(codes):
    half = jax.ShapeDtypeStruct((2,) + codes.shape[2:], jnp.float32)
    return pl.pallas_call(
        near_kernel,
        out_shape=(half, half),
        in_specs=[VMEM],
        out_specs=(VMEM, VMEM),
        compiler_params=PARAMS,
    )(codes)


def exact_dot(values, basis):
    total = None
    for step in range(3):
        head = values.astype(jnp.bfloat16)
        product = jnp.dot(head, basis, preferred_element_type=jnp.float32)
        total = product if total is None else total + product
        values = values - head.astype(jnp.float32)
    return total


def corr_kernel(codes, row_share, basis, total, corr):
    def add(i, value):
        return value + decode(codes[i])

    total[...] = row_share[...] + lax.fori_loop(
        1, codes.shape[0], add, decode(codes[0]), unroll=4
    )
    value = exact_dot(total[...], basis[...])
    for i in range(corr.shape[0]):
        corr[i] = value


def local_corr(copies, codes, row_share, basis):
    return pl.pallas_call(
        corr_kernel,
        out_shape=(
            jax.ShapeDtypeStruct(row_share.shape, jnp.float32),
            jax.ShapeDtypeStruct(
                (copies, row_share.shape[0], basis.shape[1]), jnp.float32
            ),
        ),
        in_specs=[VMEM] * 3,
        out_specs=(VMEM, VMEM),
        compiler_params=PARAMS,
    )(codes, row_share, basis)


def stack_kernel(copies, refs, out):
    at = 0
    for ref in refs:
        pieces = [ref[...]] if len(ref.shape) == 2 else [ref[i] for i in range(ref.shape[0])]
        for piece in pieces:
            for j in range(copies):
                out[j, at] = piece
            at += 1


def stack(copies, *pieces):
    count = sum(1 if piece.ndim == 2 else piece.shape[0] for piece in pieces)
    return pl.pallas_call(
        lambda *refs: stack_kernel(copies, refs[:-1], refs[-1]),
        out_shape=jax.ShapeDtypeStruct(
            (copies, count) + pieces[0].shape[-2:], pieces[0].dtype
        ),
        in_specs=[VMEM] * len(pieces),
        out_specs=VMEM,
        compiler_params=PARAMS,
    )(*pieces)


def across(value, d):
    return lax.ppermute(value, "zh", [(i, i ^ d) for i in range(4)])


def share(piece, axes, count):
    return lax.all_to_all(jnp.broadcast_to(piece[None], (count,) + piece.shape), axes, 0, 0)


def on_device(tiles, tile_rows, tile_cols, counts, vectors, basis):
    block = tiles[0, 0]
    slots, size = block.shape[:2]
    width = vectors.shape[1]
    rows, cols = tile_rows.reshape(-1), tile_cols.reshape(-1)
    ids = jnp.stack(
        [
            rows ^ lax.axis_index("zh"),
            cols,
            jnp.broadcast_to(counts.reshape(1), (slots,)),
        ]
    )
    own = vectors.T
    column_part = share(own, ROW, 32)
    third = across(own, 3)
    column_part, third = lax.optimization_barrier((column_part, third))
    middle = across(stack(1, own, third)[0], 1)
    four = stack(8, own, middle, third)
    row_codes = tile_products(forward_kernel, (8, 4), ids, block, column_part)
    along_y = lax.all_to_all(row_codes, "y", 0, 0)
    four, along_y = lax.optimization_barrier((four, along_y))
    row_part = lax.all_to_all(four, "y", 0, 0).reshape(32, width, size)
    kept, sent = sum_along_y(along_y)
    kept = kept + across(sent, 1)
    col_codes = tile_products(backward_kernel, (32,), ids, block, row_part)
    kept, col_codes = lax.optimization_barrier((kept, col_codes))
    along_row = lax.all_to_all(col_codes, ROW, 0, 0)
    row_share = kept[0] + across(kept[1], 3)
    combined, corr = local_corr(8, along_row, row_share, basis)
    corr = lax.all_to_all(corr, ("x", "c"), 0, 0).sum(0)
    corr = share(corr, "y", 8).sum(0)
    corr = share(corr, ("zl", "zh"), 16).sum(0)
    removed = lax.dot_general(
        corr,
        basis.astype(jnp.float32),
        (((1,), (1,)), ((), ())),
        precision=lax.Precision.HIGHEST,
    )
    return ((combined - removed).T, corr.T)


def solution(mesh):
    fine = Mesh(mesh.devices.reshape(SIZES), AXES)
    col = ("y", "zh")
    placed = (
        P(ROW, col, None, None, None),
        P(ROW, col, None),
        P(ROW, col, None),
        P(ROW, col),
        P(AXES, None),
        P(AXES, None),
    )
    return jax.shard_map(
        on_device,
        mesh=fine,
        in_specs=placed,
        out_specs=(P(AXES, None), P()),
        check_vma=False,
    )
```

```python
import jax
import jax.numpy as jnp
from jax import lax
from jax.experimental import pallas as pl
from jax.experimental.pallas import tpu as pltpu
from jax.sharding import Mesh, PartitionSpec as P

AXES = ("zl", "x", "c", "y", "zh")
SIZES = (4, 4, 2, 8, 4)
ROW = ("zl", "x", "c")
VMEM = pl.BlockSpec(memory_space=pltpu.VMEM)
SMEM = pl.BlockSpec(memory_space=pltpu.SMEM)
LOW = 111
PARAMS = pltpu.CompilerParams(vmem_limit_bytes=24 * 2**20)


def encode(terms):
    rows = lax.broadcasted_iota(jnp.int32, terms.shape, 0)
    top = jnp.max(jnp.abs(terms), axis=0, keepdims=True)
    power = jnp.floor(jnp.log2(jnp.maximum(top, 2.0**-LOW))) + 1.0
    power = jnp.maximum(power, -float(LOW))
    q = jnp.round(terms * jnp.exp2(14.0 - power))
    q = jnp.clip(q, -16383.0, 16383.0).astype(jnp.int32)
    stored = jnp.broadcast_to(power.astype(jnp.int32) + LOW, terms.shape)
    return (2 * q + ((stored >> rows) & 1)).astype(jnp.int16)


def decode(codes):
    codes = codes.astype(jnp.int32)
    rows = lax.broadcasted_iota(jnp.int32, codes.shape, 0)
    place = jnp.where(rows < 7, 1 << jnp.minimum(rows, 7), 0).astype(jnp.float32)
    power = jnp.sum((codes & 1).astype(jnp.float32) * place, axis=0, keepdims=True) - float(LOW)
    return (codes >> 1).astype(jnp.float32) * jnp.exp2(power - 14.0)


def products(forward, ids, tiles, part, sums):
    sums[...] = jnp.zeros_like(sums)
    for k in range(tiles.shape[0]):
        r, c = ids[0, k], ids[1, k]
        source, target, contract = (c, r, 1) if forward else (r, c, 0)
        product = lax.dot_general(
            part[source],
            tiles[k],
            (((1,), (contract,)), ((), ())),
            preferred_element_type=jnp.float32,
        )
        sums[target] = sums[target] + product * (k < ids[2, k]).astype(jnp.float32)


def forward_kernel(ids, tiles, part, codes, sums):
    products(True, ids, tiles, part, sums)

    def code(y, carry):
        for d in range(codes.shape[1]):
            codes[y, d] = encode(sums[y * codes.shape[1] + d])
        return carry

    lax.fori_loop(0, codes.shape[0], code, 0)


def backward_kernel(ids, tiles, part, codes, sums):
    products(False, ids, tiles, part, sums)

    def code(i, carry):
        codes[i] = encode(sums[i])
        return carry

    lax.fori_loop(0, sums.shape[0], code, 0, unroll=4)


def tile_products(kernel, lead, ids, tiles, part):
    return pl.pallas_call(
        kernel,
        out_shape=jax.ShapeDtypeStruct(lead + part.shape[1:], jnp.int16),
        in_specs=[SMEM, VMEM, VMEM],
        out_specs=VMEM,
        scratch_shapes=[pltpu.VMEM(part.shape, jnp.float32)],
        compiler_params=PARAMS,
        cost_estimate=pl.CostEstimate(
            flops=32 * tiles.size, bytes_accessed=4 * tiles.size, transcendentals=0
        ),
    )(ids, tiles, part)


def near_kernel(codes, kept, sent):
    for d, (ref, at) in enumerate(((kept, 0), (sent, 0), (sent, 1), (kept, 1))):
        total = decode(codes[0, d])
        for source in range(1, codes.shape[0]):
            total = total + decode(codes[source, d])
        ref[at] = total


def sum_along_y(codes):
    half = jax.ShapeDtypeStruct((2,) + codes.shape[2:], jnp.float32)
    return pl.pallas_call(
        near_kernel,
        out_shape=(half, half),
        in_specs=[VMEM],
        out_specs=(VMEM, VMEM),
        compiler_params=PARAMS,
    )(codes)


def exact_dot(values, basis):
    total = None
    for step in range(3):
        head = values.astype(jnp.bfloat16)
        product = jnp.dot(head, basis, preferred_element_type=jnp.float32)
        total = product if total is None else total + product
        values = values - head.astype(jnp.float32)
    return total


def corr_kernel(codes, kept, own_basis, third_basis, total, corr):
    def add(i, value):
        return value + decode(codes[i])

    total[...] = kept[0] + lax.fori_loop(1, codes.shape[0], add, decode(codes[0]), unroll=4)
    value = exact_dot(total[...], own_basis[...]) + exact_dot(kept[1], third_basis[...])
    for i in range(corr.shape[0]):
        corr[i] = value


def local_corr(copies, codes, kept, own_basis, third_basis):
    return pl.pallas_call(
        corr_kernel,
        out_shape=(
            jax.ShapeDtypeStruct(kept.shape[1:], jnp.float32),
            jax.ShapeDtypeStruct(
                (copies, kept.shape[1], own_basis.shape[1]), jnp.float32
            ),
        ),
        in_specs=[VMEM] * 4,
        out_specs=(VMEM, VMEM),
        compiler_params=PARAMS,
    )(codes, kept, own_basis, third_basis)


def stack_kernel(copies, refs, out):
    at = 0
    for ref in refs:
        pieces = [ref[...]] if len(ref.shape) == 2 else [ref[i] for i in range(ref.shape[0])]
        for piece in pieces:
            for j in range(copies):
                out[j, at] = piece
            at += 1


def stack(copies, *pieces):
    count = sum(1 if piece.ndim == 2 else piece.shape[0] for piece in pieces)
    return pl.pallas_call(
        lambda *refs: stack_kernel(copies, refs[:-1], refs[-1]),
        out_shape=jax.ShapeDtypeStruct(
            (copies, count) + pieces[0].shape[-2:], pieces[0].dtype
        ),
        in_specs=[VMEM] * len(pieces),
        out_specs=VMEM,
        compiler_params=PARAMS,
    )(*pieces)


def across(value, d):
    return lax.ppermute(value, "zh", [(i, i ^ d) for i in range(4)])


def share(piece, axes, count):
    return lax.all_to_all(jnp.broadcast_to(piece[None], (count,) + piece.shape), axes, 0, 0)


def on_device(tiles, tile_rows, tile_cols, counts, vectors, basis):
    block = tiles[0, 0]
    slots, size = block.shape[:2]
    width = vectors.shape[1]
    rows, cols = tile_rows.reshape(-1), tile_cols.reshape(-1)
    ids = jnp.stack(
        [
            rows ^ lax.axis_index("zh"),
            cols,
            jnp.broadcast_to(counts.reshape(1), (slots,)),
        ]
    )
    own = vectors.T
    column_part = lax.all_to_all(stack(32, own), ROW, 0, 0).reshape(32, width, size)
    third, third_basis = across(own, 3), across(basis, 3)
    column_part, third, third_basis = lax.optimization_barrier((column_part, third, third_basis))
    middle = across(stack(1, own, third)[0], 1)
    four = stack(8, own, middle, third)
    row_codes = tile_products(forward_kernel, (8, 4), ids, block, column_part)
    along_y = lax.all_to_all(row_codes, "y", 0, 0)
    four, along_y = lax.optimization_barrier((four, along_y))
    row_part = lax.all_to_all(four, "y", 0, 0).reshape(32, width, size)
    kept, sent = sum_along_y(along_y)
    kept = kept + across(sent, 1)
    col_codes = tile_products(backward_kernel, (32,), ids, block, row_part)
    kept, col_codes = lax.optimization_barrier((kept, col_codes))
    along_row = lax.all_to_all(col_codes, ROW, 0, 0)
    total, corr = local_corr(8, along_row, kept, basis, third_basis)
    combined = total + across(kept[1], 3)
    corr = lax.all_to_all(corr, ("x", "c"), 0, 0).sum(0)
    corr = share(corr, "y", 8).sum(0)
    corr = share(corr, ("zl", "zh"), 16).sum(0)
    removed = lax.dot_general(
        corr,
        basis.astype(jnp.float32),
        (((1,), (1,)), ((), ())),
        precision=lax.Precision.HIGHEST,
    )
    return ((combined - removed).T, corr.T)


def solution(mesh):
    fine = Mesh(mesh.devices.reshape(SIZES), AXES)
    col = ("y", "zh")
    placed = (
        P(ROW, col, None, None, None),
        P(ROW, col, None),
        P(ROW, col, None),
        P(ROW, col),
        P(AXES, None),
        P(AXES, None),
    )
    return jax.shard_map(
        on_device,
        mesh=fine,
        in_specs=placed,
        out_specs=(P(AXES, None), P()),
        check_vma=False,
    )
```

```python
import jax
import jax.numpy as jnp
from jax import lax
from jax.experimental import pallas as pl
from jax.experimental.pallas import tpu as pltpu
from jax.sharding import Mesh, PartitionSpec as P

AXES = ("zl", "x", "c", "y", "zh")
SIZES = (4, 4, 2, 8, 4)
ROW = ("zl", "x", "c")
VMEM = pl.BlockSpec(memory_space=pltpu.VMEM)
SMEM = pl.BlockSpec(memory_space=pltpu.SMEM)
LOW = 111
PARAMS = pltpu.CompilerParams(vmem_limit_bytes=24 * 2**20)


def encode(terms):
    rows = lax.broadcasted_iota(jnp.int32, terms.shape, 0)
    top = jnp.max(jnp.abs(terms), axis=0, keepdims=True)
    power = jnp.floor(jnp.log2(jnp.maximum(top, 2.0**-LOW))) + 1.0
    power = jnp.maximum(power, -float(LOW))
    q = jnp.round(terms * jnp.exp2(14.0 - power))
    q = jnp.clip(q, -16383.0, 16383.0).astype(jnp.int32)
    stored = jnp.broadcast_to(power.astype(jnp.int32) + LOW, terms.shape)
    return (2 * q + ((stored >> rows) & 1)).astype(jnp.int16)


def decode(codes):
    codes = codes.astype(jnp.int32)
    rows = lax.broadcasted_iota(jnp.int32, codes.shape, 0)
    place = jnp.where(rows < 7, 1 << jnp.minimum(rows, 7), 0).astype(jnp.float32)
    power = jnp.sum((codes & 1).astype(jnp.float32) * place, axis=0, keepdims=True) - float(LOW)
    return (codes >> 1).astype(jnp.float32) * jnp.exp2(power - 14.0)


def products(forward, ids, tiles, part, sums):
    sums[...] = jnp.zeros_like(sums)
    for k in range(tiles.shape[0]):
        r, c = ids[0, k], ids[1, k]
        source, target, contract = (c, r, 1) if forward else (r, c, 0)
        product = lax.dot_general(
            part[source],
            tiles[k],
            (((1,), (contract,)), ((), ())),
            preferred_element_type=jnp.float32,
        )
        sums[target] = sums[target] + product * (k < ids[2, k]).astype(jnp.float32)


def forward_kernel(ids, tiles, part, codes, sums):
    products(True, ids, tiles, part, sums)

    def code(y, carry):
        for d in range(codes.shape[1]):
            codes[y, d] = encode(sums[y * codes.shape[1] + d])
        return carry

    lax.fori_loop(0, codes.shape[0], code, 0)


def backward_kernel(ids, tiles, part, codes, sums):
    products(False, ids, tiles, part, sums)

    def code(i, carry):
        codes[i] = encode(sums[i])
        return carry

    lax.fori_loop(0, sums.shape[0], code, 0, unroll=4)


def tile_products(kernel, lead, ids, tiles, part):
    return pl.pallas_call(
        kernel,
        out_shape=jax.ShapeDtypeStruct(lead + part.shape[1:], jnp.int16),
        in_specs=[SMEM, VMEM, VMEM],
        out_specs=VMEM,
        scratch_shapes=[pltpu.VMEM(part.shape, jnp.float32)],
        compiler_params=PARAMS,
        cost_estimate=pl.CostEstimate(
            flops=32 * tiles.size, bytes_accessed=4 * tiles.size, transcendentals=0
        ),
    )(ids, tiles, part)


def near_kernel(codes, kept, sent):
    for d, (ref, at) in enumerate(((kept, 0), (sent, 0), (sent, 1), (kept, 1))):
        total = decode(codes[0, d])
        for source in range(1, codes.shape[0]):
            total = total + decode(codes[source, d])
        ref[at] = total


def sum_along_y(codes):
    half = jax.ShapeDtypeStruct((2,) + codes.shape[2:], jnp.float32)
    return pl.pallas_call(
        near_kernel,
        out_shape=(half, half),
        in_specs=[VMEM],
        out_specs=(VMEM, VMEM),
        compiler_params=PARAMS,
    )(codes)


def exact_dot(values, basis):
    total = None
    for step in range(3):
        head = values.astype(jnp.bfloat16)
        product = jnp.dot(head, basis, preferred_element_type=jnp.float32)
        total = product if total is None else total + product
        values = values - head.astype(jnp.float32)
    return total


def corr_kernel(codes, row_share, basis, total, corr):
    def add(i, value):
        return value + decode(codes[i])

    total[...] = row_share[...] + lax.fori_loop(
        1, codes.shape[0], add, decode(codes[0]), unroll=4
    )
    value = exact_dot(total[...], basis[...])
    for i in range(corr.shape[0]):
        corr[i] = value


def local_corr(copies, codes, row_share, basis):
    return pl.pallas_call(
        corr_kernel,
        out_shape=(
            jax.ShapeDtypeStruct(row_share.shape, jnp.float32),
            jax.ShapeDtypeStruct(
                (copies, row_share.shape[0], basis.shape[1]), jnp.float32
            ),
        ),
        in_specs=[VMEM] * 3,
        out_specs=(VMEM, VMEM),
        compiler_params=PARAMS,
    )(codes, row_share, basis)


def stack_kernel(copies, refs, out):
    at = 0
    for ref in refs:
        pieces = [ref[...]] if len(ref.shape) == 2 else [ref[i] for i in range(ref.shape[0])]
        for piece in pieces:
            for j in range(copies):
                out[j, at] = piece
            at += 1


def stack(copies, *pieces):
    count = sum(1 if piece.ndim == 2 else piece.shape[0] for piece in pieces)
    return pl.pallas_call(
        lambda *refs: stack_kernel(copies, refs[:-1], refs[-1]),
        out_shape=jax.ShapeDtypeStruct(
            (copies, count) + pieces[0].shape[-2:], pieces[0].dtype
        ),
        in_specs=[VMEM] * len(pieces),
        out_specs=VMEM,
        compiler_params=PARAMS,
    )(*pieces)


def copy_kernel(source, target):
    for k in range(source.shape[0]):
        target[k] = source[k]


def staged(tiles):
    return pl.pallas_call(
        copy_kernel,
        out_shape=jax.ShapeDtypeStruct(tiles.shape, tiles.dtype),
        in_specs=[VMEM],
        out_specs=VMEM,
        compiler_params=PARAMS,
    )(tiles)


def across(value, d):
    return lax.ppermute(value, "zh", [(i, i ^ d) for i in range(4)])


def share(piece, axes, count):
    return lax.all_to_all(jnp.broadcast_to(piece[None], (count,) + piece.shape), axes, 0, 0)


def on_device(tiles, tile_rows, tile_cols, counts, vectors, basis):
    block = tiles[0, 0]
    slots, size = block.shape[:2]
    width = vectors.shape[1]
    rows, cols = tile_rows.reshape(-1), tile_cols.reshape(-1)
    ids = jnp.stack(
        [
            rows ^ lax.axis_index("zh"),
            cols,
            jnp.broadcast_to(counts.reshape(1), (slots,)),
        ]
    )
    own = vectors.T
    column_part = share(own, ROW, 32)
    third = across(own, 3)
    column_part, third, block = lax.optimization_barrier((column_part, third, staged(block)))
    middle = across(stack(1, own, third)[0], 1)
    four = stack(8, own, middle, third)
    row_codes = tile_products(forward_kernel, (8, 4), ids, block, column_part)
    along_y = lax.all_to_all(row_codes, "y", 0, 0)
    four, along_y = lax.optimization_barrier((four, along_y))
    row_part = lax.all_to_all(four, "y", 0, 0).reshape(32, width, size)
    kept, sent = sum_along_y(along_y)
    kept = kept + across(sent, 1)
    col_codes = tile_products(backward_kernel, (32,), ids, block, row_part)
    kept, col_codes = lax.optimization_barrier((kept, col_codes))
    along_row = lax.all_to_all(col_codes, ROW, 0, 0)
    row_share = kept[0] + across(kept[1], 3)
    combined, corr = local_corr(8, along_row, row_share, basis)
    corr = lax.all_to_all(corr, ("x", "c"), 0, 0).sum(0)
    corr = share(corr, "y", 8).sum(0)
    corr = share(corr, ("zl", "zh"), 16).sum(0)
    removed = lax.dot_general(
        corr,
        basis.astype(jnp.float32),
        (((1,), (1,)), ((), ())),
        precision=lax.Precision.HIGHEST,
    )
    return ((combined - removed).T, corr.T)


def solution(mesh):
    fine = Mesh(mesh.devices.reshape(SIZES), AXES)
    col = ("y", "zh")
    placed = (
        P(ROW, col, None, None, None),
        P(ROW, col, None),
        P(ROW, col, None),
        P(ROW, col),
        P(AXES, None),
        P(AXES, None),
    )
    return jax.shard_map(
        on_device,
        mesh=fine,
        in_specs=placed,
        out_specs=(P(AXES, None), P()),
        check_vma=False,
    )
```

```python
import jax
import jax.numpy as jnp
from jax import lax
from jax.experimental import pallas as pl
from jax.experimental.pallas import tpu as pltpu
from jax.sharding import Mesh, PartitionSpec as P

AXES = ("zl", "x", "c", "y", "zh")
SIZES = (4, 4, 2, 8, 4)
ROW = ("zl", "x", "c")
VMEM = pl.BlockSpec(memory_space=pltpu.VMEM)
SMEM = pl.BlockSpec(memory_space=pltpu.SMEM)
LOW = 111
PARAMS = pltpu.CompilerParams(vmem_limit_bytes=24 * 2**20)


def encode(terms):
    rows = lax.broadcasted_iota(jnp.int32, terms.shape, 0)
    top = jnp.max(jnp.abs(terms), axis=0, keepdims=True)
    power = jnp.floor(jnp.log2(jnp.maximum(top, 2.0**-LOW))) + 1.0
    power = jnp.maximum(power, -float(LOW))
    q = jnp.round(terms * jnp.exp2(14.0 - power))
    q = jnp.clip(q, -16383.0, 16383.0).astype(jnp.int32)
    stored = jnp.broadcast_to(power.astype(jnp.int32) + LOW, terms.shape)
    return (2 * q + ((stored >> rows) & 1)).astype(jnp.int16)


def decode(codes):
    codes = codes.astype(jnp.int32)
    rows = lax.broadcasted_iota(jnp.int32, codes.shape, 0)
    place = jnp.where(rows < 7, 1 << jnp.minimum(rows, 7), 0).astype(jnp.float32)
    power = jnp.sum((codes & 1).astype(jnp.float32) * place, axis=0, keepdims=True) - float(LOW)
    return (codes >> 1).astype(jnp.float32) * jnp.exp2(power - 14.0)


def products(forward, ids, tiles, part, sums):
    sums[...] = jnp.zeros_like(sums)
    for k in range(tiles.shape[0]):
        r, c = ids[0, k], ids[1, k]
        source, target, contract = (c, r, 1) if forward else (r, c, 0)
        product = lax.dot_general(
            part[source],
            tiles[k],
            (((1,), (contract,)), ((), ())),
            preferred_element_type=jnp.float32,
        )
        sums[target] = sums[target] + product * (k < ids[2, k]).astype(jnp.float32)


def forward_kernel(ids, tiles, part, codes, sums):
    products(True, ids, tiles, part, sums)

    def code(y, carry):
        for d in range(codes.shape[1]):
            codes[y, d] = encode(sums[y * codes.shape[1] + d])
        return carry

    lax.fori_loop(0, codes.shape[0], code, 0)


def backward_kernel(ids, tiles, part, codes, sums):
    products(False, ids, tiles, part, sums)

    def code(i, carry):
        codes[i] = encode(sums[i])
        return carry

    lax.fori_loop(0, sums.shape[0], code, 0, unroll=4)


def tile_products(kernel, lead, ids, tiles, part):
    return pl.pallas_call(
        kernel,
        out_shape=jax.ShapeDtypeStruct(lead + part.shape[1:], jnp.int16),
        in_specs=[SMEM, VMEM, VMEM],
        out_specs=VMEM,
        scratch_shapes=[pltpu.VMEM(part.shape, jnp.float32)],
        compiler_params=PARAMS,
        cost_estimate=pl.CostEstimate(
            flops=32 * tiles.size, bytes_accessed=4 * tiles.size, transcendentals=0
        ),
    )(ids, tiles, part)


def near_kernel(codes, kept, sent):
    for d, (ref, at) in enumerate(((kept, 0), (sent, 0), (sent, 1), (kept, 1))):
        total = decode(codes[0, d])
        for source in range(1, codes.shape[0]):
            total = total + decode(codes[source, d])
        ref[at] = total


def sum_along_y(codes):
    half = jax.ShapeDtypeStruct((2,) + codes.shape[2:], jnp.float32)
    return pl.pallas_call(
        near_kernel,
        out_shape=(half, half),
        in_specs=[VMEM],
        out_specs=(VMEM, VMEM),
        compiler_params=PARAMS,
    )(codes)


def exact_dot(values, basis):
    total = None
    for step in range(3):
        head = values.astype(jnp.bfloat16)
        product = jnp.dot(head, basis, preferred_element_type=jnp.float32)
        total = product if total is None else total + product
        values = values - head.astype(jnp.float32)
    return total


def corr_kernel(codes, row_share, basis, total, corr):
    def add(i, value):
        return value + decode(codes[i])

    total[...] = row_share[...] + lax.fori_loop(
        1, codes.shape[0], add, decode(codes[0]), unroll=4
    )
    value = exact_dot(total[...], basis[...])
    for i in range(corr.shape[0]):
        corr[i] = value


def local_corr(copies, codes, row_share, basis):
    return pl.pallas_call(
        corr_kernel,
        out_shape=(
            jax.ShapeDtypeStruct(row_share.shape, jnp.float32),
            jax.ShapeDtypeStruct(
                (copies, row_share.shape[0], basis.shape[1]), jnp.float32
            ),
        ),
        in_specs=[VMEM] * 3,
        out_specs=(VMEM, VMEM),
        compiler_params=PARAMS,
    )(codes, row_share, basis)


def stack_kernel(copies, refs, out):
    at = 0
    for ref in refs:
        pieces = [ref[...]] if len(ref.shape) == 2 else [ref[i] for i in range(ref.shape[0])]
        for piece in pieces:
            for j in range(copies):
                out[j, at] = piece
            at += 1


def stack(copies, *pieces):
    count = sum(1 if piece.ndim == 2 else piece.shape[0] for piece in pieces)
    return pl.pallas_call(
        lambda *refs: stack_kernel(copies, refs[:-1], refs[-1]),
        out_shape=jax.ShapeDtypeStruct(
            (copies, count) + pieces[0].shape[-2:], pieces[0].dtype
        ),
        in_specs=[VMEM] * len(pieces),
        out_specs=VMEM,
        compiler_params=PARAMS,
    )(*pieces)


def copy_kernel(source, target):
    for k in range(source.shape[0]):
        target[k] = source[k]


def staged(tiles):
    return pl.pallas_call(
        copy_kernel,
        out_shape=jax.ShapeDtypeStruct(tiles.shape, tiles.dtype),
        in_specs=[VMEM],
        out_specs=VMEM,
        compiler_params=PARAMS,
    )(tiles)


def across(value, d):
    return lax.ppermute(value, "zh", [(i, i ^ d) for i in range(4)])


def share(piece, axes, count):
    return lax.all_to_all(jnp.broadcast_to(piece[None], (count,) + piece.shape), axes, 0, 0)


def on_device(tiles, tile_rows, tile_cols, counts, vectors, basis):
    block = tiles[0, 0]
    slots, size = block.shape[:2]
    width = vectors.shape[1]
    rows, cols = tile_rows.reshape(-1), tile_cols.reshape(-1)
    ids = jnp.stack(
        [
            rows ^ lax.axis_index("zh"),
            cols,
            jnp.broadcast_to(counts.reshape(1), (slots,)),
        ]
    )
    own = vectors.T
    column_part = share(own, ROW, 32)
    third = across(own, 3)
    column_part, block = lax.optimization_barrier((column_part, staged(block)))
    row_codes = tile_products(forward_kernel, (8, 4), ids, block, column_part)
    row_codes, third = lax.optimization_barrier((row_codes, third))
    middle = across(stack(1, own, third)[0], 1)
    four = stack(8, own, middle, third)
    along_y = lax.all_to_all(row_codes, "y", 0, 0)
    four, along_y = lax.optimization_barrier((four, along_y))
    row_part = lax.all_to_all(four, "y", 0, 0).reshape(32, width, size)
    kept, sent = sum_along_y(along_y)
    received = across(sent, 1)
    col_codes = tile_products(backward_kernel, (32,), ids, block, row_part)
    received, col_codes = lax.optimization_barrier((received, col_codes))
    along_row = lax.all_to_all(col_codes, ROW, 0, 0)
    kept = kept + received
    row_share = kept[0] + across(kept[1], 3)
    combined, corr = local_corr(8, along_row, row_share, basis)
    corr = lax.all_to_all(corr, ("x", "c"), 0, 0).sum(0)
    corr = share(corr, "y", 8).sum(0)
    corr = share(corr, ("zl", "zh"), 16).sum(0)
    removed = lax.dot_general(
        corr,
        basis.astype(jnp.float32),
        (((1,), (1,)), ((), ())),
        precision=lax.Precision.HIGHEST,
    )
    return ((combined - removed).T, corr.T)


def solution(mesh):
    fine = Mesh(mesh.devices.reshape(SIZES), AXES)
    col = ("y", "zh")
    placed = (
        P(ROW, col, None, None, None),
        P(ROW, col, None),
        P(ROW, col, None),
        P(ROW, col),
        P(AXES, None),
        P(AXES, None),
    )
    return jax.shard_map(
        on_device,
        mesh=fine,
        in_specs=placed,
        out_specs=(P(AXES, None), P()),
        check_vma=False,
    )
```

```python
import jax
import jax.numpy as jnp
from jax import lax
from jax.experimental import pallas as pl
from jax.experimental.pallas import tpu as pltpu
from jax.sharding import Mesh, PartitionSpec as P

AXES = ("zl", "x", "c", "y", "zh")
SIZES = (4, 4, 2, 8, 4)
ROW = ("zl", "x", "c")
VMEM = pl.BlockSpec(memory_space=pltpu.VMEM)
SMEM = pl.BlockSpec(memory_space=pltpu.SMEM)
LOW = 111
PARAMS = pltpu.CompilerParams(vmem_limit_bytes=24 * 2**20)


def encode(terms):
    rows = lax.broadcasted_iota(jnp.int32, terms.shape, 0)
    top = jnp.max(jnp.abs(terms), axis=0, keepdims=True)
    power = jnp.floor(jnp.log2(jnp.maximum(top, 2.0**-LOW))) + 1.0
    power = jnp.maximum(power, -float(LOW))
    q = jnp.round(terms * jnp.exp2(14.0 - power))
    q = jnp.clip(q, -16383.0, 16383.0).astype(jnp.int32)
    stored = jnp.broadcast_to(power.astype(jnp.int32) + LOW, terms.shape)
    return (2 * q + ((stored >> rows) & 1)).astype(jnp.int16)


def decode(codes):
    codes = codes.astype(jnp.int32)
    rows = lax.broadcasted_iota(jnp.int32, codes.shape, 0)
    place = jnp.where(rows < 7, 1 << jnp.minimum(rows, 7), 0).astype(jnp.float32)
    power = jnp.sum((codes & 1).astype(jnp.float32) * place, axis=0, keepdims=True) - float(LOW)
    return (codes >> 1).astype(jnp.float32) * jnp.exp2(power - 14.0)


def products(forward, ids, tiles, part, sums):
    sums[...] = jnp.zeros_like(sums)
    for k in range(tiles.shape[0]):
        r, c = ids[0, k], ids[1, k]
        source, target, contract = (c, r, 1) if forward else (r, c, 0)
        product = lax.dot_general(
            part[source],
            tiles[k],
            (((1,), (contract,)), ((), ())),
            preferred_element_type=jnp.float32,
        )
        sums[target] = sums[target] + product * (k < ids[2, k]).astype(jnp.float32)


def forward_kernel(ids, tiles, part, codes, sums):
    products(True, ids, tiles, part, sums)

    def code(y, carry):
        for d in range(codes.shape[1]):
            codes[y, d] = encode(sums[y * codes.shape[1] + d])
        return carry

    lax.fori_loop(0, codes.shape[0], code, 0)


def backward_kernel(ids, tiles, part, codes, sums):
    products(False, ids, tiles, part, sums)

    def code(i, carry):
        codes[i] = encode(sums[i])
        return carry

    lax.fori_loop(0, sums.shape[0], code, 0, unroll=4)


def tile_products(kernel, lead, ids, tiles, part):
    return pl.pallas_call(
        kernel,
        out_shape=jax.ShapeDtypeStruct(lead + part.shape[1:], jnp.int16),
        in_specs=[SMEM, VMEM, VMEM],
        out_specs=VMEM,
        scratch_shapes=[pltpu.VMEM(part.shape, jnp.float32)],
        compiler_params=PARAMS,
        cost_estimate=pl.CostEstimate(
            flops=32 * tiles.size, bytes_accessed=4 * tiles.size, transcendentals=0
        ),
    )(ids, tiles, part)


def near_kernel(codes, kept, sent):
    for d, (ref, at) in enumerate(((kept, 0), (sent, 0), (sent, 1), (kept, 1))):
        total = decode(codes[0, d])
        for source in range(1, codes.shape[0]):
            total = total + decode(codes[source, d])
        ref[at] = total


def sum_along_y(codes):
    half = jax.ShapeDtypeStruct((2,) + codes.shape[2:], jnp.float32)
    return pl.pallas_call(
        near_kernel,
        out_shape=(half, half),
        in_specs=[VMEM],
        out_specs=(VMEM, VMEM),
        compiler_params=PARAMS,
    )(codes)


def exact_dot(values, basis):
    total = None
    for step in range(3):
        head = values.astype(jnp.bfloat16)
        product = jnp.dot(head, basis, preferred_element_type=jnp.float32)
        total = product if total is None else total + product
        values = values - head.astype(jnp.float32)
    return total


def corr_kernel(codes, row_share, basis, total, corr):
    def add(i, value):
        return value + decode(codes[i])

    total[...] = row_share[...] + lax.fori_loop(
        1, codes.shape[0], add, decode(codes[0]), unroll=4
    )
    value = exact_dot(total[...], basis[...])
    for i in range(corr.shape[0]):
        corr[i] = value


def local_corr(copies, codes, row_share, basis):
    return pl.pallas_call(
        corr_kernel,
        out_shape=(
            jax.ShapeDtypeStruct(row_share.shape, jnp.float32),
            jax.ShapeDtypeStruct(
                (copies, row_share.shape[0], basis.shape[1]), jnp.float32
            ),
        ),
        in_specs=[VMEM] * 3,
        out_specs=(VMEM, VMEM),
        compiler_params=PARAMS,
    )(codes, row_share, basis)


def stack_kernel(copies, refs, out):
    at = 0
    for ref in refs:
        pieces = [ref[...]] if len(ref.shape) == 2 else [ref[i] for i in range(ref.shape[0])]
        for piece in pieces:
            for j in range(copies):
                out[j, at] = piece
            at += 1


def stack(copies, *pieces):
    count = sum(1 if piece.ndim == 2 else piece.shape[0] for piece in pieces)
    return pl.pallas_call(
        lambda *refs: stack_kernel(copies, refs[:-1], refs[-1]),
        out_shape=jax.ShapeDtypeStruct(
            (copies, count) + pieces[0].shape[-2:], pieces[0].dtype
        ),
        in_specs=[VMEM] * len(pieces),
        out_specs=VMEM,
        compiler_params=PARAMS,
    )(*pieces)


def copy_kernel(source, target):
    for k in range(source.shape[0]):
        target[k] = source[k]


def staged(tiles):
    return pl.pallas_call(
        copy_kernel,
        out_shape=jax.ShapeDtypeStruct(tiles.shape, tiles.dtype),
        in_specs=[VMEM],
        out_specs=VMEM,
        compiler_params=PARAMS,
    )(tiles)


def across(value, d):
    return lax.ppermute(value, "zh", [(i, i ^ d) for i in range(4)])


def share(piece, axes, count):
    return lax.all_to_all(jnp.broadcast_to(piece[None], (count,) + piece.shape), axes, 0, 0)


def on_device(tiles, tile_rows, tile_cols, counts, vectors, basis):
    block = tiles[0, 0]
    slots, size = block.shape[:2]
    width = vectors.shape[1]
    rows, cols = tile_rows.reshape(-1), tile_cols.reshape(-1)
    ids = jnp.stack(
        [
            rows ^ lax.axis_index("zh"),
            cols,
            jnp.broadcast_to(counts.reshape(1), (slots,)),
        ]
    )
    own = vectors.T
    column_part = share(own, ROW, 32)
    third = across(own, 3)
    column_part, block = lax.optimization_barrier((column_part, staged(block)))
    row_codes = tile_products(forward_kernel, (8, 4), ids, block, column_part)
    row_codes, third = lax.optimization_barrier((row_codes, third))
    middle = across(stack(1, own, third)[0], 1)
    four = stack(8, own, middle, third)
    along_y = lax.all_to_all(row_codes, "y", 0, 0)
    four, along_y = lax.optimization_barrier((four, along_y))
    row_part = lax.all_to_all(four, "y", 0, 0).reshape(32, width, size)
    kept, sent = sum_along_y(along_y)
    received = across(sent, 1)
    col_codes = tile_products(backward_kernel, (32,), ids, block, row_part)
    received, col_codes = lax.optimization_barrier((received, col_codes))
    along_row = lax.all_to_all(col_codes, ROW, 0, 0)
    kept = kept + received
    row_share = kept[0] + across(kept[1], 3)
    combined, corr = local_corr(8, along_row, row_share, basis)
    corr = lax.all_to_all(corr, ("x", "c"), 0, 0).sum(0)
    corr = share(corr, ("zl", "zh"), 16).sum(0)
    corr = share(corr, "y", 8).sum(0)
    removed = lax.dot_general(
        corr,
        basis.astype(jnp.float32),
        (((1,), (1,)), ((), ())),
        precision=lax.Precision.HIGHEST,
    )
    return ((combined - removed).T, corr.T)


def solution(mesh):
    fine = Mesh(mesh.devices.reshape(SIZES), AXES)
    col = ("y", "zh")
    placed = (
        P(ROW, col, None, None, None),
        P(ROW, col, None),
        P(ROW, col, None),
        P(ROW, col),
        P(AXES, None),
        P(AXES, None),
    )
    return jax.shard_map(
        on_device,
        mesh=fine,
        in_specs=placed,
        out_specs=(P(AXES, None), P()),
        check_vma=False,
    )
```
